32 devices in a mesh: dp: 16 (over z, y, x), mp: 2 (over core).
Axes of the slice: x: 2, y: 2, z: 4, core: 2. Of those that a mesh axis runs over, the one named last changes fastest.
Arguments:
- query_grad: bfloat16 [2048, 7168], P('mp', 'dp'), may hold values from -6 to 6
- basis_in: bfloat16 [2048, 2048], P(None, 'mp'), may hold values from -0.125 to 0.125
- basis_out: bfloat16 [7168, 7168], P('mp', 'dp'), may hold values from -0.0625 to 0.0625
- eigen_scales: float32 [2048, 7168], P('mp', 'dp'), may hold values from 0.006 to 240
- inputs: bfloat16 [8192, 2048], P('dp', 'mp'), may hold values from -6 to 6
- out_grads: bfloat16 [8192, 7168], P('dp', 'mp'), may hold values from -0.00015258789 to 0.00015258789
- segment_ids: int32 [8192], P('dp'), may hold values from 0 to 31, as said below
Outputs:
- sequence_scores: float32 [32], P('dp')
The draws below stay inside these ranges and needn't reach their ends.
Inputs may be any that keep to these rules, and one draw needn't show every extreme that they name: `segment_ids`: the tokens of each index of dp form 2 runs of one or more tokens, each run one whole sequence; sequence numbers are given to the runs in an arbitrary order, each number to exactly one run.
All inputs are finite; a program needn't handle non-finite values.
Results may differ from the reference program's by a relative error of at most 0.024.
Values may be sent and summed in bfloat16 or wider, within the bound.
A program may use at most 128 MiB of HBM per device.

```python
import math
import jax
import jax.numpy as jnp
from jax import lax

D = 2048
F = 7168
TOK_DEV = 512
SEQ_DEV = 2
TOKENS = 8192
SEQS = 32


def draw_eigen_scales(key, part):
    key = jax.random.fold_in(key, 7)
    level_key = jax.random.fold_in(key, 11)
    block_key = jax.random.fold_in(key, 13)
    level = jax.random.uniform(level_key, (D, F), jnp.float32, math.log(0.05), 0.0)
    block_level = jax.random.uniform(block_key, (4, 8), jnp.float32, -2.0, 2.0)
    row_block = jnp.arange(D, dtype=jnp.int32) * 4 // D
    col_block = jnp.arange(F, dtype=jnp.int32) * 8 // F
    row_pick = (row_block[:, None] == jnp.arange(4, dtype=jnp.int32)[None, :]).astype(jnp.float32)
    col_pick = (col_block[:, None] == jnp.arange(8, dtype=jnp.int32)[None, :]).astype(jnp.float32)
    row_levels = jnp.sum(row_pick[:, :, None] * block_level[None, :, :], axis=1)
    block_field = jnp.sum(row_levels[:, None, :] * col_pick[None, :, :], axis=2)
    row_place = jnp.arange(D, dtype=jnp.float32)[:, None] / D
    col_place = jnp.arange(F, dtype=jnp.float32)[None, :] / F
    rising = jnp.exp(math.log(10.0) * (0.5 * row_place + 0.5 * col_place))
    return jnp.exp(level + block_field) * rising


def draw_segment_ids(key, part):
    key = jax.random.fold_in(key, 5)
    holders = TOKENS // TOK_DEV
    cut_key = jax.random.fold_in(key, 1)
    order_key = jax.random.fold_in(key, 2)
    cuts = jax.random.randint(cut_key, (holders,), 1, TOK_DEV, dtype=jnp.int32)
    local = (jnp.arange(TOK_DEV, dtype=jnp.int32)[None, :] >= cuts[:, None]).astype(jnp.int32)
    run_slot = jnp.arange(holders, dtype=jnp.int32)[:, None] * SEQ_DEV + local
    order = jax.random.permutation(order_key, SEQS).astype(jnp.int32)
    target = SEQS // 2
    where_target = jnp.argmax((order == target).astype(jnp.int32)).astype(jnp.int32)
    places = jnp.arange(SEQS, dtype=jnp.int32)
    first_value = order[0]
    order = jnp.where(places == 0, target, jnp.where(places == where_target, first_value, order))
    return order[run_slot].reshape(TOKENS).astype(jnp.int32)


def shard_levels(rng, dims, cuts, low, largest):
    factor_of = 1.0
    for position, shards_of in cuts:
        steps = jax.random.uniform(jax.random.fold_in(jax.random.fold_in(rng, 6), position), (shards_of,), jnp.float32, low / len(cuts), largest / len(cuts))
        factor_of = factor_of * jnp.repeat(jnp.exp(steps), dims[position] // shards_of).reshape((-1,) + (1,) * (len(dims) - 1 - position))
    return factor_of


def normal_values(rng, shape, width, most, cuts=(), held_as=jnp.bfloat16):
    result = width * jax.random.normal(rng, shape, jnp.float32)
    if cuts:
        result = result * shard_levels(rng, shape, cuts, -0.22, 0.18)
    return jnp.clip(result, -most, most).astype(held_as)


def setup_inputs(seed: int = 0) -> dict:
    splits = jax.random.split(jax.random.key(seed), 8)
    query_grad = normal_values(splits[0], (D, F), 1.0, 6.0, ((0, 2), (1, 16)))
    basis_in = normal_values(splits[1], (D, D), D ** -0.5, 0.125, ((1, 2),))
    basis_out = normal_values(splits[2], (F, F), F ** -0.5, 0.0625, ((0, 2), (1, 16)))
    eigen_scales = draw_eigen_scales(jax.random.fold_in(splits[7], 71), 0)
    inputs = normal_values(splits[4], (TOKENS, D), 1.0, 6.0, ((0, 16), (1, 2)))
    out_grads = normal_values(splits[5], (TOKENS, F), 0.00001, 0.00015258789, ((0, 16), (1, 2)))
    segment_ids = draw_segment_ids(jax.random.fold_in(splits[7], 71), 0)
    return dict(query_grad=query_grad, basis_in=basis_in, basis_out=basis_out, eigen_scales=eigen_scales, inputs=inputs, out_grads=out_grads, segment_ids=segment_ids)


damping_ratio = 0.1


def reference(query_grad, basis_in, basis_out, eigen_scales, inputs, out_grads, segment_ids):
    turned = jnp.dot(query_grad, basis_out, preferred_element_type=jnp.float32).astype(jnp.bfloat16)
    rotated = jnp.dot(basis_in.T, turned, preferred_element_type=jnp.float32)
    damping = damping_ratio * jnp.sum(eigen_scales) / (D * F)
    rescaled = (rotated / (eigen_scales + damping)).astype(jnp.bfloat16)
    back = jnp.dot(rescaled, basis_out.T, preferred_element_type=jnp.float32).astype(jnp.bfloat16)
    projected = jnp.dot(inputs, basis_in, preferred_element_type=jnp.float32)
    pulled = jnp.dot(out_grads, back.T, preferred_element_type=jnp.float32)
    token_score = jnp.sum(projected * pulled, axis=1)
    onehot = (segment_ids[:, None] == jnp.arange(SEQS, dtype=jnp.int32)[None, :]).astype(jnp.float32)
    return jnp.dot(token_score, onehot, precision=lax.Precision.HIGHEST)
```

```python
import jax
import jax.numpy as jnp
from jax import lax
from jax.sharding import PartitionSpec as P

IN = 4
damping_ratio = 0.1
BF = jnp.bfloat16
F32 = jnp.float32


def on_device(query_grad, basis_in, basis_out, eigen_scales, inputs, out_grads, segment_ids):
    n = lax.axis_size("dp")
    outer = n // IN
    d_in = basis_in.shape[0]
    fc = basis_out.shape[1]
    f_all = fc * n
    tok = inputs.shape[0]
    me = lax.axis_index("dp")
    o, p = me // IN, me % IN

    def swap(v, j):
        return lax.ppermute(v, "dp", [(i, i ^ j) for i in range(n)])

    def right(v):
        return lax.ppermute(v, "dp", [(i, i + IN) for i in range(n - IN)])

    def left(v):
        return lax.ppermute(v, "dp", [(i, i - IN) for i in range(IN, n)])

    def line_gather(v):
        rights, lefts = [], []
        a = b = v
        for _ in range(outer - 1):
            a, b = right(a), left(b)
            rights.append(a)
            lefts.append(b)
        held = jnp.stack(rights[::-1] + [v] + lefts)
        return lax.dynamic_slice_in_dim(held, outer - 1 - o, outer, axis=0)

    part_sum = jnp.broadcast_to(jnp.sum(eigen_scales), (1, 128))
    sums = lax.all_gather(part_sum, ("dp", "mp"), axis=0, tiled=True)
    damping = damping_ratio * jnp.sum(sums[:, 0]) / (d_in * f_all)

    w_full = lax.all_gather(query_grad, "mp", axis=0, tiled=True)
    u = lax.dot_general(
        basis_in, w_full, (((0,), (0,)), ((), ())), preferred_element_type=F32
    ).astype(BF)
    u_all = line_gather(u)

    rows = basis_out.reshape(-1, IN, fc, fc)
    q = []
    for j in range(IN):
        sent = lax.dynamic_index_in_dim(rows, p ^ j, axis=1, keepdims=False)
        got = swap(sent, j) if j else sent
        q.append(lax.all_gather(got, "mp", axis=0, tiled=True))

    terms = {}
    for j in (3, 1, 2, 0):
        y = lax.dot_general(u_all, q[j], (((0, 2), (0, 1)), ((), ())), preferred_element_type=F32)
        terms[j] = swap(y.astype(BF), j).astype(F32) if j else y
    rotated = terms[0] + terms[1] + terms[2] + terms[3]
    rescaled = (rotated / (eigen_scales + damping)).astype(BF)

    res = [swap(rescaled, j) if j else rescaled for j in range(IN)]
    q_cat = jnp.concatenate(q, axis=2)
    res_cat = jnp.concatenate(res, axis=1)
    part = lax.dot_general(
        q_cat, res_cat, (((2,), (1,)), ((), ())), preferred_element_type=F32
    ).astype(BF)

    def block(k):
        return lax.dynamic_index_in_dim(part, k % outer, axis=0, keepdims=False).astype(F32)

    a = b = None
    for t in range(outer - 1):
        va = block(outer - 1 - t + o)
        vb = block(o + t + 1)
        if a is not None:
            va, vb = va + a, vb + b
        a = right(va.astype(BF)).astype(F32)
        b = left(vb.astype(BF)).astype(F32)
    back = (block(o) + a + b).astype(BF)
    back_all = line_gather(back)

    x_full = lax.all_gather(inputs, "mp", axis=1, tiled=True)
    proj = jnp.dot(x_full, basis_in, preferred_element_type=F32)
    proj_bf = proj.astype(BF)
    proj_all = jnp.concatenate([proj] + [swap(proj_bf, j).astype(F32) for j in range(1, IN)])
    cols = out_grads.reshape(tok, -1, IN, fc)
    g = []
    for j in range(IN):
        sent = lax.dynamic_index_in_dim(cols, p ^ j, axis=2, keepdims=False).transpose(1, 0, 2)
        g.append(swap(sent, j) if j else sent)
    g_all = lax.all_gather(jnp.concatenate(g, axis=1), "mp", axis=0, tiled=True)
    ids = jnp.concatenate([segment_ids] + [swap(segment_ids, j) for j in range(1, IN)])

    pulled = lax.dot_general(
        g_all, back_all, (((0, 2), (0, 1)), ((), ())), preferred_element_type=F32
    )
    score = jnp.sum(proj_all * pulled, axis=1)
    seq_count = 2 * n
    onehot = (ids[:, None] == jnp.arange(seq_count, dtype=jnp.int32)[None, :]).astype(F32)
    seq_terms = jnp.dot(score, onehot, precision=lax.Precision.HIGHEST)
    every = lax.all_gather(seq_terms[None], ("dp", "mp"), axis=0, tiled=True)
    return lax.dynamic_slice_in_dim(jnp.sum(every, axis=0), 2 * me, 2)


def solution(mesh):
    return jax.shard_map(
        on_device,
        mesh=mesh,
        in_specs=(
            P("mp", "dp"),
            P(None, "mp"),
            P("mp", "dp"),
            P("mp", "dp"),
            P("dp", "mp"),
            P("dp", "mp"),
            P("dp"),
        ),
        out_specs=P("dp"),
        check_vma=False,
    )
```

```python
import jax
import jax.numpy as jnp
from jax import lax
from jax.experimental.layout import Layout, with_layout_constraint
from jax.sharding import PartitionSpec as P

IN = 4
damping_ratio = 0.1
BF = jnp.bfloat16
F32 = jnp.float32


def on_device(query_grad, basis_in, basis_out, eigen_scales, inputs, out_grads, segment_ids):
    n = lax.axis_size("dp")
    outer = n // IN
    d_in = basis_in.shape[0]
    fc = basis_out.shape[1]
    f_all = fc * n
    tok = inputs.shape[0]
    me = lax.axis_index("dp")
    o, p = me // IN, me % IN

    def swap(v, j):
        return lax.ppermute(v, "dp", [(i, i ^ j) for i in range(n)])

    def right(v):
        return lax.ppermute(v, "dp", [(i, i + IN) for i in range(n - IN)])

    def left(v):
        return lax.ppermute(v, "dp", [(i, i - IN) for i in range(IN, n)])

    def beside(pair, extras):
        moved = [swap(x, j) for x, j in extras]
        return lax.optimization_barrier((pair, moved))

    def line_gather(v, extras):
        rights, lefts = [v], [v]
        moved = []
        for t in range(outer - 1):
            pair = (right(rights[-1]), left(lefts[-1]))
            if t < len(extras):
                pair, arrived = beside(pair, extras[t])
                moved += arrived
            rights.append(pair[0])
            lefts.append(pair[1])
        blocks = [v] + [jnp.where(s <= o, rights[s], lefts[outer - s]) for s in range(1, outer)]
        return blocks, moved

    def sum_over_devices(v):
        v = v + sum(swap(v, j) for j in range(1, IN))
        shifts = [
            lax.ppermute(v, "dp", [(i, (i + s * IN) % n) for i in range(n)])
            for s in range(1, outer)
        ]
        v = v + sum(shifts)
        m = lax.axis_size("mp")
        others = [
            lax.ppermute(v, "mp", [(i, (i + s) % m) for i in range(m)]) for s in range(1, m)
        ]
        return v + sum(others)

    def pick(gathered, s):
        k = (o - s) % outer
        per = gathered.shape[1]
        part = lax.dynamic_index_in_dim(gathered, k // per, axis=0, keepdims=False)
        return lax.dynamic_index_in_dim(part, k % per, axis=0, keepdims=False)

    w_full = lax.all_gather(query_grad, "mp", axis=0, tiled=True)
    u = lax.dot_general(
        basis_in, w_full, (((0,), (0,)), ((), ())), preferred_element_type=F32
    ).astype(BF)
    rows = with_layout_constraint(basis_out, Layout(major_to_minor=(0, 1)))
    rows, u = lax.optimization_barrier((rows, u))
    rows = rows.reshape(-1, IN, fc, fc)
    sends = [lax.dynamic_index_in_dim(rows, p ^ j, axis=1, keepdims=False) for j in range(IN)]
    u_rel, got = line_gather(u, [[(sends[1], 1), (sends[2], 2)], [(sends[3], 3)]])
    got = [sends[0]] + got
    q_all = lax.all_gather(jnp.stack(got, axis=1), "mp", axis=0)
    q_rel = jnp.stack([pick(q_all, s) for s in range(outer)])

    part_sum = jnp.broadcast_to(jnp.sum(eigen_scales), (8, 128))
    damping = damping_ratio * sum_over_devices(part_sum)[:1, :1] / (d_in * f_all)
    u_cat = jnp.concatenate(u_rel, axis=1)
    u_cat, q_rel, damping = lax.optimization_barrier((u_cat, q_rel, damping))

    terms = {}
    for j in (3, 1, 2, 0):
        y = jnp.dot(u_cat, q_rel[:, j].reshape(-1, fc), preferred_element_type=F32)
        terms[j] = swap(y.astype(BF), j).astype(F32) if j else y
    rotated = terms[0] + terms[1] + terms[2] + terms[3]
    rescaled = (rotated / (eigen_scales + damping)).astype(BF)

    res = jnp.stack([swap(rescaled, j) if j else rescaled for j in range(IN)])

    def block(s):
        return lax.dot_general(
            q_rel[s], res, (((0, 2), (0, 2)), ((), ())), preferred_element_type=F32
        )

    x_full = lax.all_gather(inputs, "mp", axis=1, tiled=True)
    proj = jnp.dot(x_full, basis_in, preferred_element_type=F32).astype(BF)
    cols = out_grads.reshape(tok, -1, IN, fc)
    g_sends = [
        lax.dynamic_index_in_dim(cols, p ^ j, axis=2, keepdims=False).transpose(1, 0, 2)
        for j in range(IN)
    ]
    res, proj, g_sends = lax.optimization_barrier((res, proj, g_sends))
    extras = [
        [(g_sends[1], 1), (g_sends[2], 2)],
        [(g_sends[3], 3)],
        [(proj, 1), (proj, 2)],
    ]
    a = b = None
    moved = []
    for t in range(outer - 1):
        va, vb = block(t + 1), block(outer - 1 - t)
        if a is not None:
            va, vb = va + a, vb + b
        a, b = right(va.astype(BF)), left(vb.astype(BF))
        if t < len(extras):
            (a, b), arrived = beside((a, b), extras[t])
            moved += arrived
        a, b = a.astype(F32), b.astype(F32)
    back = (block(0) + a + b).astype(BF)

    g = [g_sends[0]] + moved[:3]
    back_rel, last = line_gather(back, [[(proj, 3)]])
    g_all = lax.all_gather(jnp.concatenate(g, axis=1), "mp", axis=0)
    projs = [proj] + moved[3:] + last
    ids = jnp.concatenate([segment_ids] + [swap(segment_ids, j) for j in range(1, IN)])
    back_rel, projs = lax.optimization_barrier((back_rel, projs))
    proj_all = jnp.concatenate(projs)
    score = 0.0
    for s in range(outer):
        pulled = lax.dot_general(
            pick(g_all, s), back_rel[s], (((1,), (0,)), ((), ())), preferred_element_type=F32
        )
        score = score + jnp.sum(proj_all.astype(F32) * pulled, axis=1)
    seq_count = 2 * n
    onehot = (ids[:, None] == jnp.arange(seq_count, dtype=jnp.int32)[None, :]).astype(F32)
    seq_terms = jnp.dot(score, onehot, precision=lax.Precision.HIGHEST)
    return lax.dynamic_slice_in_dim(sum_over_devices(seq_terms), 2 * me, 2)


def solution(mesh):
    return jax.shard_map(
        on_device,
        mesh=mesh,
        in_specs=(
            P("mp", "dp"),
            P(None, "mp"),
            P("mp", "dp"),
            P("mp", "dp"),
            P("dp", "mp"),
            P("dp", "mp"),
            P("dp"),
        ),
        out_specs=P("dp"),
        check_vma=False,
    )
```

```python
import jax
import jax.numpy as jnp
from jax import lax
from jax.experimental.layout import Layout, with_layout_constraint
from jax.sharding import PartitionSpec as P

IN = 4
damping_ratio = 0.1
BF = jnp.bfloat16
F32 = jnp.float32


def on_device(query_grad, basis_in, basis_out, eigen_scales, inputs, out_grads, segment_ids):
    n = lax.axis_size("dp")
    outer = n // IN
    d_in = basis_in.shape[0]
    fc = basis_out.shape[1]
    f_all = fc * n
    tok = inputs.shape[0]
    me = lax.axis_index("dp")
    o, p = me // IN, me % IN

    def swap(v, j):
        return lax.ppermute(v, "dp", [(i, i ^ j) for i in range(n)])

    def right(v):
        return lax.ppermute(v, "dp", [(i, i + IN) for i in range(n - IN)])

    def left(v):
        return lax.ppermute(v, "dp", [(i, i - IN) for i in range(IN, n)])

    def beside(pair, extras, later):
        moved = [swap(x, j) for x, j in extras]
        waiting = [[x for x, _ in step] for step in later]
        pair, moved, waiting = lax.optimization_barrier((pair, moved, waiting))
        later = [[(x, j) for x, (_, j) in zip(xs, step)] for xs, step in zip(waiting, later)]
        return pair, moved, later

    def halves(v, axis):
        return jnp.split(v, 2, axis=axis)

    def plane_rest(from_x, from_y, axis):
        first = swap(halves(from_y, axis)[0], 1)
        second = swap(halves(from_x, axis)[1], 2)
        return jnp.concatenate([first, second], axis=axis)

    def line_gather(v, extras, tail=None):
        rights, lefts = [v], [v]
        moved = []
        for t in range(outer - 1):
            pair = (right(rights[-1]), left(lefts[-1]))
            if extras:
                pair, arrived, extras = beside(pair, extras[0], extras[1:])
                moved += arrived
            if tail is not None and t == outer - 2:
                pair, kept = lax.optimization_barrier((pair, tail(moved)))
                moved = (moved, kept)
            rights.append(pair[0])
            lefts.append(pair[1])
        blocks = [v] + [jnp.where(s <= o, rights[s], lefts[outer - s]) for s in range(1, outer)]
        return blocks, moved

    def sum_over_devices(v):
        v = v + sum(swap(v, j) for j in range(1, IN))
        shifts = [
            lax.ppermute(v, "dp", [(i, (i + s * IN) % n) for i in range(n)])
            for s in range(1, outer)
        ]
        v = v + sum(shifts)
        m = lax.axis_size("mp")
        others = [
            lax.ppermute(v, "mp", [(i, (i + s) % m) for i in range(m)]) for s in range(1, m)
        ]
        return v + sum(others)

    def pick(gathered, s):
        k = (o - s) % outer
        per = gathered.shape[1]
        part = lax.dynamic_index_in_dim(gathered, k // per, axis=0, keepdims=False)
        return lax.dynamic_index_in_dim(part, k % per, axis=0, keepdims=False)

    w_full = lax.all_gather(query_grad, "mp", axis=0, tiled=True)
    u = lax.dot_general(
        basis_in, w_full, (((0,), (0,)), ((), ())), preferred_element_type=F32
    ).astype(BF)
    rows = with_layout_constraint(basis_out, Layout(major_to_minor=(0, 1)))
    rows, u = lax.optimization_barrier((rows, u))
    rows = rows.reshape(-1, IN, fc, fc)
    sends = [lax.dynamic_index_in_dim(rows, p ^ j, axis=1, keepdims=False) for j in range(IN)]
    x_full = lax.all_gather(inputs, "mp", axis=1, tiled=True)
    proj = jnp.dot(x_full, basis_in, preferred_element_type=F32).astype(BF)

    def prepare(got):
        q_all = lax.all_gather(jnp.stack([sends[0]] + got[:3], axis=1), "mp", axis=0)
        q_rel = jnp.stack([pick(q_all, s) for s in range(outer)])
        part_sum = jnp.broadcast_to(jnp.sum(eigen_scales), (8, 128))
        damping = damping_ratio * sum_over_devices(part_sum)[:1, :1] / (d_in * f_all)
        return q_rel, damping

    u_rel, (got, (q_rel, damping)) = line_gather(
        u,
        [[(sends[1], 1), (sends[2], 2)], [(sends[3], 3)], [(proj, 1), (proj, 2)]],
        prepare,
    )
    proj_x, proj_y = got[3:]
    u_cat = jnp.concatenate(u_rel, axis=1)

    def term(j):
        return jnp.dot(u_cat, q_rel[:, j].reshape(-1, fc), preferred_element_type=F32)

    far = halves(term(3).astype(BF), 0)
    far_y = swap(far[0], 1).astype(F32)
    far_x = swap(far[1], 2).astype(F32)
    term_y = halves(term(2), 0)
    term_x = halves(term(1), 0)
    term_y = jnp.concatenate([term_y[0] + far_y, term_y[1]])
    term_x = jnp.concatenate([term_x[0], term_x[1] + far_x])
    own = term(0)
    got_x, got_y = swap(term_x.astype(BF), 1), swap(term_y.astype(BF), 2)
    rotated = own + got_x.astype(F32) + got_y.astype(F32)
    rescaled = (rotated / (eigen_scales + damping)).astype(BF)

    res_x, res_y = swap(rescaled, 1), swap(rescaled, 2)
    res = jnp.stack([rescaled, res_x, res_y, plane_rest(res_x, res_y, 0)])

    def block(s):
        return lax.dot_general(
            q_rel[s], res, (((0, 2), (0, 2)), ((), ())), preferred_element_type=F32
        )

    cols = out_grads.reshape(tok, -1, IN, fc)
    g_sends = [
        lax.dynamic_index_in_dim(cols, p ^ j, axis=2, keepdims=False).transpose(1, 0, 2)
        for j in range(IN)
    ]
    res, g_sends = lax.optimization_barrier((res, g_sends))
    extras = [
        [(g_sends[1], 1), (g_sends[2], 2)],
        [(g_sends[3], 3)],
        [(halves(proj_y, 0)[0], 1), (halves(proj_x, 0)[1], 2)],
    ]
    a = b = None
    moved = []
    for t in range(outer - 1):
        va, vb = block(t + 1), block(outer - 1 - t)
        if a is not None:
            va, vb = va + a, vb + b
        a, b = right(va.astype(BF)), left(vb.astype(BF))
        if extras:
            (a, b), arrived, extras = beside((a, b), extras[0], extras[1:])
            moved += arrived
        a, b = a.astype(F32), b.astype(F32)
    back = (block(0) + a + b).astype(BF)

    g = [g_sends[0]] + moved[:3]
    back_rel, _ = line_gather(back, [])
    g_all = lax.all_gather(jnp.concatenate(g, axis=1), "mp", axis=0)
    projs = [proj, proj_x, proj_y] + moved[3:]
    ids = jnp.concatenate([segment_ids] + [swap(segment_ids, j) for j in range(1, IN)])
    proj_all = jnp.concatenate(projs)
    score = 0.0
    for s in range(outer):
        pulled = lax.dot_general(
            pick(g_all, s), back_rel[s], (((1,), (0,)), ((), ())), preferred_element_type=F32
        )
        score = score + jnp.sum(proj_all.astype(F32) * pulled, axis=1)
    seq_count = 2 * n
    onehot = (ids[:, None] == jnp.arange(seq_count, dtype=jnp.int32)[None, :]).astype(F32)
    seq_terms = jnp.dot(score, onehot, precision=lax.Precision.HIGHEST)
    return lax.dynamic_slice_in_dim(sum_over_devices(seq_terms), 2 * me, 2)


def solution(mesh):
    return jax.shard_map(
        on_device,
        mesh=mesh,
        in_specs=(
            P("mp", "dp"),
            P(None, "mp"),
            P("mp", "dp"),
            P("mp", "dp"),
            P("dp", "mp"),
            P("dp", "mp"),
            P("dp"),
        ),
        out_specs=P("dp"),
        check_vma=False,
    )
```

```python
import jax
import jax.numpy as jnp
from jax import lax
from jax.experimental.layout import Layout, with_layout_constraint
from jax.sharding import PartitionSpec as P

IN = 4
damping_ratio = 0.1
BF = jnp.bfloat16
F32 = jnp.float32


def on_device(query_grad, basis_in, basis_out, eigen_scales, inputs, out_grads, segment_ids):
    n = lax.axis_size("dp")
    outer = n // IN
    d_in = basis_in.shape[0]
    fc = basis_out.shape[1]
    f_all = fc * n
    tok = inputs.shape[0]
    me = lax.axis_index("dp")
    o, p = me // IN, me % IN

    def swap(v, j):
        return lax.ppermute(v, "dp", [(i, i ^ j) for i in range(n)])

    def right(v):
        return lax.ppermute(v, "dp", [(i, i + IN) for i in range(n - IN)])

    def left(v):
        return lax.ppermute(v, "dp", [(i, i - IN) for i in range(IN, n)])

    def beside(pair, extras, later):
        moved = [swap(x, j) for x, j in extras]
        waiting = [[x for x, _ in step] for step in later]
        pair, moved, waiting = lax.optimization_barrier((pair, moved, waiting))
        later = [[(x, j) for x, (_, j) in zip(xs, step)] for xs, step in zip(waiting, later)]
        return pair, moved, later

    def halves(v, axis):
        return jnp.split(v, 2, axis=axis)

    def plane_rest(from_x, from_y, axis):
        first = swap(halves(from_y, axis)[0], 1)
        second = swap(halves(from_x, axis)[1], 2)
        return jnp.concatenate([first, second], axis=axis)

    def line_gather(v, extras, tail=None, rounds=(), state=None):
        rights, lefts = [v], [v]
        moved = []
        for t in range(outer - 1):
            pair = (right(rights[-1]), left(lefts[-1]))
            if extras:
                pair, arrived, extras = beside(pair, extras[0], extras[1:])
                moved += arrived
            if t < len(rounds):
                pair, state = lax.optimization_barrier((pair, rounds[t](state)))
            if tail is not None and t == outer - 2:
                pair, kept = lax.optimization_barrier((pair, tail(moved, state)))
                moved = (moved, kept)
            rights.append(pair[0])
            lefts.append(pair[1])
        blocks = [v] + [jnp.where(s <= o, rights[s], lefts[outer - s]) for s in range(1, outer)]
        return blocks, moved

    def over_plane(v):
        return v + sum(swap(v, j) for j in range(1, IN))

    def over_line(v):
        shifts = [
            lax.ppermute(v, "dp", [(i, (i + s * IN) % n) for i in range(n)])
            for s in range(1, outer)
        ]
        return v + sum(shifts)

    def over_cores(v):
        m = lax.axis_size("mp")
        others = [
            lax.ppermute(v, "mp", [(i, (i + s) % m) for i in range(m)]) for s in range(1, m)
        ]
        return v + sum(others)

    def sum_over_devices(v):
        return over_cores(over_line(over_plane(v)))

    def pick(gathered, s):
        k = (o - s) % outer
        per = gathered.shape[1]
        part = lax.dynamic_index_in_dim(gathered, k // per, axis=0, keepdims=False)
        return lax.dynamic_index_in_dim(part, k % per, axis=0, keepdims=False)

    w_full = lax.all_gather(query_grad, "mp", axis=0, tiled=True)
    u = lax.dot_general(
        basis_in, w_full, (((0,), (0,)), ((), ())), preferred_element_type=F32
    ).astype(BF)
    rows = with_layout_constraint(basis_out, Layout(major_to_minor=(0, 1)))
    rows, u = lax.optimization_barrier((rows, u))
    rows = rows.reshape(-1, IN, fc, fc)
    sends = [lax.dynamic_index_in_dim(rows, p ^ j, axis=1, keepdims=False) for j in range(IN)]
    x_full = lax.all_gather(inputs, "mp", axis=1, tiled=True)
    proj = jnp.dot(x_full, basis_in, preferred_element_type=F32).astype(BF)

    def prepare(got, scale_sum):
        q_all = lax.all_gather(jnp.stack([sends[0]] + got[:3], axis=1), "mp", axis=0)
        q_rel = jnp.stack([pick(q_all, s) for s in range(outer)])
        return q_rel, damping_ratio * scale_sum[:1, :1] / (d_in * f_all)

    u_rel, (got, (q_rel, damping)) = line_gather(
        u,
        [[(sends[1], 1), (sends[2], 2)], [(sends[3], 3)] + [(segment_ids, j) for j in range(1, IN)],
         [(proj, 1), (proj, 2)]],
        prepare,
        (over_plane, over_line, over_cores),
        jnp.broadcast_to(jnp.sum(eigen_scales), (8, 128)),
    )
    ids = jnp.concatenate([segment_ids] + got[3:6])
    proj_x, proj_y = got[6:]
    u_cat = jnp.concatenate(u_rel, axis=1)

    def term(j):
        return jnp.dot(u_cat, q_rel[:, j].reshape(-1, fc), preferred_element_type=F32)

    far = halves(term(3).astype(BF), 0)
    far_y = swap(far[0], 1).astype(F32)
    far_x = swap(far[1], 2).astype(F32)
    term_y = halves(term(2), 0)
    term_x = halves(term(1), 0)
    term_y = jnp.concatenate([term_y[0] + far_y, term_y[1]])
    term_x = jnp.concatenate([term_x[0], term_x[1] + far_x])
    own = term(0)
    got_x, got_y = swap(term_x.astype(BF), 1), swap(term_y.astype(BF), 2)
    rotated = own + got_x.astype(F32) + got_y.astype(F32)
    rescaled = (rotated / (eigen_scales + damping)).astype(BF)

    res_x, res_y = swap(rescaled, 1), swap(rescaled, 2)
    res = jnp.stack([rescaled, res_x, res_y, plane_rest(res_x, res_y, 0)])

    def block(s):
        return lax.dot_general(
            q_rel[s], res, (((0, 2), (0, 2)), ((), ())), preferred_element_type=F32
        )

    cols = out_grads.reshape(tok, -1, IN, fc)
    g_sends = [
        lax.dynamic_index_in_dim(cols, p ^ j, axis=2, keepdims=False).transpose(1, 0, 2)
        for j in range(IN)
    ]
    res, g_sends = lax.optimization_barrier((res, g_sends))
    extras = [
        [(g_sends[1], 1), (g_sends[2], 2)],
        [(g_sends[3], 3)],
        [(halves(proj_y, 0)[0], 1), (halves(proj_x, 0)[1], 2)],
    ]
    a = b = None
    moved = []
    for t in range(outer - 1):
        va, vb = block(t + 1), block(outer - 1 - t)
        if a is not None:
            va, vb = va + a, vb + b
        a, b = right(va.astype(BF)), left(vb.astype(BF))
        if extras:
            (a, b), arrived, extras = beside((a, b), extras[0], extras[1:])
            moved += arrived
        a, b = a.astype(F32), b.astype(F32)
    back = (block(0) + a + b).astype(BF)

    g = [g_sends[0]] + moved[:3]
    back_rel, _ = line_gather(back, [])
    g_all = lax.all_gather(jnp.concatenate(g, axis=1), "mp", axis=0)
    projs = [proj, proj_x, proj_y] + moved[3:]
    proj_all = jnp.concatenate(projs)
    score = 0.0
    for s in range(outer):
        pulled = lax.dot_general(
            pick(g_all, s), back_rel[s], (((1,), (0,)), ((), ())), preferred_element_type=F32
        )
        score = score + jnp.sum(proj_all.astype(F32) * pulled, axis=1)
    seq_count = 2 * n
    onehot = (ids[:, None] == jnp.arange(seq_count, dtype=jnp.int32)[None, :]).astype(F32)
    seq_terms = jnp.dot(score, onehot, precision=lax.Precision.HIGHEST)
    return lax.dynamic_slice_in_dim(sum_over_devices(seq_terms), 2 * me, 2)


def solution(mesh):
    return jax.shard_map(
        on_device,
        mesh=mesh,
        in_specs=(
            P("mp", "dp"),
            P(None, "mp"),
            P("mp", "dp"),
            P("mp", "dp"),
            P("dp", "mp"),
            P("dp", "mp"),
            P("dp"),
        ),
        out_specs=P("dp"),
        check_vma=False,
    )
```

```python
import jax
import jax.numpy as jnp
from jax import lax
from jax.experimental.layout import Layout, with_layout_constraint
from jax.sharding import PartitionSpec as P

IN = 4
damping_ratio = 0.1
BF = jnp.bfloat16
F32 = jnp.float32


def on_device(query_grad, basis_in, basis_out, eigen_scales, inputs, out_grads, segment_ids):
    n = lax.axis_size("dp")
    outer = n // IN
    d_in = basis_in.shape[0]
    fc = basis_out.shape[1]
    f_all = fc * n
    tok = inputs.shape[0]
    me = lax.axis_index("dp")
    o, p = me // IN, me % IN

    def swap(v, j):
        return lax.ppermute(v, "dp", [(i, i ^ j) for i in range(n)])

    def right(v):
        return lax.ppermute(v, "dp", [(i, i + IN) for i in range(n - IN)])

    def left(v):
        return lax.ppermute(v, "dp", [(i, i - IN) for i in range(IN, n)])

    def beside(pair, extras, later):
        moved = [swap(x, j) for x, j in extras]
        waiting = [[x for x, _ in step] for step in later]
        pair, moved, waiting = lax.optimization_barrier((pair, moved, waiting))
        later = [[(x, j) for x, (_, j) in zip(xs, step)] for xs, step in zip(waiting, later)]
        return pair, moved, later

    def halves(v, axis):
        return jnp.split(v, 2, axis=axis)

    def plane_rest(from_x, from_y, axis):
        first = swap(halves(from_y, axis)[0], 1)
        second = swap(halves(from_x, axis)[1], 2)
        return jnp.concatenate([first, second], axis=axis)

    def line_gather(v, extras, tail=None, rounds=(), state=None):
        rights, lefts = [v], [v]
        moved = []
        for t in range(outer - 1):
            pair = (right(rights[-1]), left(lefts[-1]))
            if extras:
                pair, arrived, extras = beside(pair, extras[0], extras[1:])
                moved += arrived
            if t < len(rounds):
                pair, state = lax.optimization_barrier((pair, rounds[t](state)))
            if tail is not None and t == outer - 2:
                pair, kept = lax.optimization_barrier((pair, tail(moved, state)))
                moved = (moved, kept)
            rights.append(pair[0])
            lefts.append(pair[1])
        blocks = [v] + [jnp.where(s <= o, rights[s], lefts[outer - s]) for s in range(1, outer)]
        return blocks, moved

    def over_plane(v):
        return v + sum(swap(v, j) for j in range(1, IN))

    def over_line(v):
        shifts = [
            lax.ppermute(v, "dp", [(i, (i + s * IN) % n) for i in range(n)])
            for s in range(1, outer)
        ]
        return v + sum(shifts)

    def over_cores(v):
        m = lax.axis_size("mp")
        others = [
            lax.ppermute(v, "mp", [(i, (i + s) % m) for i in range(m)]) for s in range(1, m)
        ]
        return v + sum(others)

    def sum_over_devices(v):
        return over_cores(over_line(over_plane(v)))

    def pick(gathered, s):
        k = (o - s) % outer
        per = gathered.shape[1]
        part = lax.dynamic_index_in_dim(gathered, k // per, axis=0, keepdims=False)
        return lax.dynamic_index_in_dim(part, k % per, axis=0, keepdims=False)

    w_full = lax.all_gather(query_grad, "mp", axis=0, tiled=True)
    u = lax.dot_general(
        basis_in, w_full, (((0,), (0,)), ((), ())), preferred_element_type=F32
    ).astype(BF)
    rows = with_layout_constraint(basis_out, Layout(major_to_minor=(0, 1)))
    rows, u = lax.optimization_barrier((rows, u))
    rows = rows.reshape(-1, IN, fc, fc)
    sends = [lax.dynamic_index_in_dim(rows, p ^ j, axis=1, keepdims=False) for j in range(IN)]
    x_full = lax.all_gather(inputs, "mp", axis=1, tiled=True)
    proj = jnp.dot(x_full, basis_in, preferred_element_type=F32).astype(BF)

    def prepare(got, scale_sum):
        q_all = lax.all_gather(jnp.stack([sends[0]] + got[:3], axis=1), "mp", axis=0)
        q_rel = jnp.stack([pick(q_all, s) for s in range(outer)])
        return q_rel, damping_ratio * scale_sum[:1, :1] / (d_in * f_all)

    u_rel, (got, (q_rel, damping)) = line_gather(
        u,
        [[(sends[1], 1), (sends[2], 2)], [(sends[3], 3)],
         [(segment_ids, j) for j in range(1, IN)] + [(proj, 1), (proj, 2)]],
        prepare,
        (over_plane, over_line, over_cores),
        jnp.broadcast_to(jnp.sum(eigen_scales), (8, 128)),
    )
    ids = jnp.concatenate([segment_ids] + got[3:6])
    proj_x, proj_y = got[6:]
    u_cat = jnp.concatenate(u_rel, axis=1)

    def term(j):
        return jnp.dot(u_cat, q_rel[:, j].reshape(-1, fc), preferred_element_type=F32)

    far = halves(term(3).astype(BF), 0)
    far_y = swap(far[0], 1).astype(F32)
    far_x = swap(far[1], 2).astype(F32)
    term_y = halves(term(2), 0)
    term_x = halves(term(1), 0)
    term_y = jnp.concatenate([term_y[0] + far_y, term_y[1]])
    term_x = jnp.concatenate([term_x[0], term_x[1] + far_x])
    own = term(0)
    got_x, got_y = swap(term_x.astype(BF), 1), swap(term_y.astype(BF), 2)
    rotated = own + got_x.astype(F32) + got_y.astype(F32)
    rescaled = (rotated / (eigen_scales + damping)).astype(BF)

    res_x, res_y = swap(rescaled, 1), swap(rescaled, 2)
    res = jnp.stack([rescaled, res_x, res_y, plane_rest(res_x, res_y, 0)])

    def block(s):
        return lax.dot_general(
            q_rel[s], res, (((0, 2), (0, 2)), ((), ())), preferred_element_type=F32
        )

    cols = out_grads.reshape(tok, -1, IN, fc)
    g_sends = [
        lax.dynamic_index_in_dim(cols, p ^ j, axis=2, keepdims=False).transpose(1, 0, 2)
        for j in range(IN)
    ]
    res, g_sends = lax.optimization_barrier((res, g_sends))
    extras = [
        [(g_sends[1], 1), (g_sends[2], 2)],
        [(g_sends[3], 3)],
        [(halves(proj_y, 0)[0], 1), (halves(proj_x, 0)[1], 2)],
    ]
    a = b = None
    moved = []
    for t in range(outer - 1):
        va, vb = block(t + 1), block(outer - 1 - t)
        if a is not None:
            va, vb = va + a, vb + b
        a, b = right(va.astype(BF)), left(vb.astype(BF))
        if extras:
            (a, b), arrived, extras = beside((a, b), extras[0], extras[1:])
            moved += arrived
        a, b = a.astype(F32), b.astype(F32)
    back = (block(0) + a + b).astype(BF)

    g = [g_sends[0]] + moved[:3]
    back_rel, _ = line_gather(back, [])
    g_all = lax.all_gather(jnp.concatenate(g, axis=1), "mp", axis=0)
    projs = [proj, proj_x, proj_y] + moved[3:]
    proj_all = jnp.concatenate(projs)
    score = 0.0
    for s in range(outer):
        pulled = lax.dot_general(
            pick(g_all, s), back_rel[s], (((1,), (0,)), ((), ())), preferred_element_type=F32
        )
        score = score + jnp.sum(proj_all.astype(F32) * pulled, axis=1)
    seq_count = 2 * n
    onehot = (ids[:, None] == jnp.arange(seq_count, dtype=jnp.int32)[None, :]).astype(F32)
    seq_terms = jnp.dot(score, onehot, precision=lax.Precision.HIGHEST)
    return lax.dynamic_slice_in_dim(sum_over_devices(seq_terms), 2 * me, 2)


def solution(mesh):
    return jax.shard_map(
        on_device,
        mesh=mesh,
        in_specs=(
            P("mp", "dp"),
            P(None, "mp"),
            P("mp", "dp"),
            P("mp", "dp"),
            P("dp", "mp"),
            P("dp", "mp"),
            P("dp"),
        ),
        out_specs=P("dp"),
        check_vma=False,
    )
```
